128 devices in a mesh: seq: 16 (over y, z_lo, core), fsdp: 8 (over x, z_hi).
Axes of the slice: x: 4, y: 4, z: 4 (z_hi: 2, z_lo: 2; z = z_hi * 2 + z_lo), core: 2. Of those that a mesh axis runs over, the one named last changes fastest.
Arguments:
- queries: bfloat16 [8, 3456, 2048], P('fsdp', 'seq'), may hold values from -5 to 5
- key_vectors: bfloat16 [8, 3456, 2048], P('fsdp', 'seq'), may hold values from -5 to 5
- values: bfloat16 [8, 3456, 2048], P('fsdp', 'seq'), may hold values from -5 to 5
- out_weight: bfloat16 [2048, 2048], P(('seq', 'fsdp')), may hold values from -0.125 to 0.125
- cotangent: bfloat16 [8, 3456, 2048], P('fsdp', 'seq'), may hold values from -0.59765625 to 0.59765625
- neighbours: int32 [18, 9], replicated, may hold values from 0 to 17, as said below
- tile_order: int32 [3456], replicated, may hold values from 0 to 3455, as said below
Outputs:
- projected: bfloat16 [8, 3456, 2048], P('fsdp', 'seq')
- grad_queries: bfloat16 [8, 3456, 2048], P('fsdp', 'seq')
- grad_keys: bfloat16 [8, 3456, 2048], P('fsdp', 'seq')
- grad_values: bfloat16 [8, 3456, 2048], P('fsdp', 'seq')
- grad_weight: bfloat16 [2048, 2048], P(('seq', 'fsdp'))
The draws below stay inside these ranges and needn't reach their ends.
Inputs may be any that keep to these rules, and one draw needn't show every extreme that they name: `neighbours`: each row names 9 different tiles, the row's own tile among them. `tile_order`: a permutation of the 3456 token indices.
All inputs are finite; a program needn't handle non-finite values.
Results may differ from the reference program's by a relative error of at most 0.014.
Values may be sent and summed in bfloat16 or wider, within the bound.
No kernel may reach another device: no remote copies, remote signals or barrier semaphores. Data moves between devices by JAX's collectives and lax.ppermute only.
A program may use at most 128 MiB of HBM per device.

```python
import math
import jax
import jax.numpy as jnp
from jax import lax

HD = 128
HEADS = 16
OUT = 2048
TILE = 192
NB = 9
BATCH = 8
TOKENS = 3456
NTILES = 18


def make_order(key):
    return jax.random.permutation(jax.random.fold_in(key, 71), TOKENS).astype(jnp.int32)


def draw_queries(key, part):
    key = jax.random.fold_in(key, 1)
    sampled = jnp.clip(jax.random.normal(key, (BATCH, TOKENS, HEADS * HD)), -5.0, 5.0)
    return sampled.astype(jnp.bfloat16)


def draw_key_vectors(key, part):
    key = jax.random.fold_in(key, 2)
    sampled = jnp.clip(jax.random.normal(key, (BATCH, TOKENS, HEADS * HD)), -5.0, 5.0)
    return sampled.astype(jnp.bfloat16)


def draw_tile_order(key, part):
    return make_order(key)


def draw_neighbours(key, part):
    key = jax.random.fold_in(key, 5)
    offset_key, order_key = jax.random.split(key)
    grid_rows = NTILES // 3
    tile_index = jnp.arange(NTILES, dtype=jnp.int32)
    offsets = jax.random.randint(offset_key, (NTILES,), -1, 2, dtype=jnp.int32)
    window_start = jnp.clip(tile_index // 3 + offsets - 1, 0, grid_rows - 3)
    window_rows = window_start[:, None] + jnp.arange(3, dtype=jnp.int32)[None, :]
    listed = (window_rows[:, :, None] * 3 + jnp.arange(3, dtype=jnp.int32)[None, None, :]).reshape(NTILES, NB)
    row_keys = jax.random.split(order_key, NTILES)
    shuffles = jax.vmap(lambda row_key: jax.random.permutation(row_key, NB))(row_keys).astype(jnp.int32)
    mixed = jnp.take_along_axis(listed, shuffles, axis=1)
    return mixed.astype(jnp.int32)


def steps_of(own_key, shape, cuts, low, high):
    gain, own = 1.0, jax.random.fold_in(own_key, 6)
    for axis_at, blocks in cuts:
        heights = jnp.exp(jax.random.uniform(jax.random.fold_in(own, axis_at), (blocks,), jnp.float32, low / len(cuts), high / len(cuts)))
        gain = gain * jnp.repeat(heights, shape[axis_at] // blocks).reshape([-1 if axis == axis_at else 1 for axis in range(len(shape))])
    return gain


def bell_draw(key, extent, width, limit, cuts=(), kind=jnp.bfloat16):
    values = jax.random.normal(key, extent, jnp.float32) * width
    if len(cuts) > 0:
        values = steps_of(key, extent, cuts, -0.22, 0.18) * values
    return jnp.clip(values, min=-limit, max=limit).astype(kind)


def setup_inputs(seed: int = 0) -> dict:
    keys = jax.random.split(jax.random.key(seed), 8)
    queries = draw_queries(jax.random.fold_in(keys[7], 71), 0)
    key_vectors = draw_key_vectors(jax.random.fold_in(keys[7], 71), 0)
    values = bell_draw(keys[2], (BATCH, TOKENS, HEADS * HD), 1.0, 5.0, ((0, 8), (1, 16)))
    out_weight = bell_draw(keys[3], (HEADS * HD, OUT), (HEADS * HD) ** -0.5, 0.125, ((0, 128),))
    cotangent = bell_draw(keys[4], (BATCH, TOKENS, OUT), 0.1, 0.59765625, ((0, 8), (1, 16)))
    neighbours = draw_neighbours(jax.random.fold_in(keys[7], 71), 0)
    tile_order = draw_tile_order(jax.random.fold_in(keys[7], 71), 0)
    return {"queries": queries, "key_vectors": key_vectors, "values": values, "out_weight": out_weight, "cotangent": cotangent, "neighbours": neighbours, "tile_order": tile_order}


def pick_tiles(tile_rows, chosen):
    gathered = tile_rows[chosen]
    return gathered.reshape(chosen.shape[0], chosen.shape[1] * tile_rows.shape[1], tile_rows.shape[2])

def head_forward(query_rows, key_rows, value_rows, tile_order, neighbours):
    count_tiles = neighbours.shape[0]
    head_width = query_rows.shape[1]
    score_scale = 1.0 / math.sqrt(head_width)
    query_tiles = query_rows[tile_order].reshape(count_tiles // 3, 3, TILE, head_width)
    key_tiles = key_rows[tile_order].reshape(count_tiles, TILE, head_width)
    value_tiles = value_rows[tile_order].reshape(count_tiles, TILE, head_width)
    chosen = neighbours.reshape(count_tiles // 3, 3, NB)

    def one_group(operands):
        query_block, pick_list = operands
        key_block = pick_tiles(key_tiles, pick_list).astype(jnp.float32)
        value_block = pick_tiles(value_tiles, pick_list).astype(jnp.float32)
        scores = jnp.einsum('gqd,gkd->gqk', query_block.astype(jnp.float32), key_block) * score_scale
        row_max = lax.optimization_barrier(jnp.max(scores, axis=-1, keepdims=True))
        row_sum = lax.optimization_barrier(jnp.sum(jnp.exp(scores - row_max), axis=-1, keepdims=True))
        log_total = row_max + jnp.log(row_sum)
        probability = jnp.exp(scores - log_total)
        low_prob = probability.astype(jnp.bfloat16)
        result = jnp.einsum('gqk,gkd->gqd', low_prob.astype(jnp.float32), value_block).astype(jnp.bfloat16)
        return (result, log_total[..., 0])
    results, log_total = lax.map(one_group, (query_tiles, chosen))
    restored = jnp.zeros(query_rows.shape, jnp.bfloat16).at[tile_order].set(results.reshape(-1, head_width))
    return (restored, log_total.reshape(-1))

def head_backward(query_rows, key_rows, value_rows, grad_rows, log_total, tile_order, neighbours):
    count_tiles = neighbours.shape[0]
    head_width = query_rows.shape[1]
    score_scale = 1.0 / math.sqrt(head_width)
    query_tiles = query_rows[tile_order].reshape(count_tiles // 3, 3, TILE, head_width)
    grad_tiles = grad_rows[tile_order].reshape(count_tiles // 3, 3, TILE, head_width)
    key_tiles = key_rows[tile_order].reshape(count_tiles, TILE, head_width)
    value_tiles = value_rows[tile_order].reshape(count_tiles, TILE, head_width)
    log_blocks = log_total.reshape(count_tiles // 3, 3, TILE)
    chosen = neighbours.reshape(count_tiles // 3, 3, NB)

    def one_group(partial_value, operands):
        key_acc, value_acc = partial_value
        query_block, grad_block, log_block, pick_list = operands
        key_block = pick_tiles(key_tiles, pick_list).astype(jnp.float32)
        value_block = pick_tiles(value_tiles, pick_list).astype(jnp.float32)
        query_wide = query_block.astype(jnp.float32)
        grad_wide = grad_block.astype(jnp.float32)
        scores = jnp.einsum('gqd,gkd->gqk', query_wide, key_block) * score_scale
        probability = jnp.exp(scores - log_block[..., None])
        low_prob = probability.astype(jnp.bfloat16)
        grad_prob = jnp.einsum('gqd,gkd->gqk', grad_wide, value_block)
        row_dot = lax.optimization_barrier(jnp.sum(probability * grad_prob, axis=-1, keepdims=True))
        grad_score = (probability * (grad_prob - row_dot)).astype(jnp.bfloat16)
        score_wide = grad_score.astype(jnp.float32)
        grad_query = (jnp.einsum('gqk,gkd->gqd', score_wide, key_block) * score_scale).astype(jnp.bfloat16)
        grad_key = jnp.einsum('gqk,gqd->gkd', score_wide, query_wide) * score_scale
        grad_value = jnp.einsum('gqk,gqd->gkd', low_prob.astype(jnp.float32), grad_wide)
        flat_ids = pick_list.reshape(-1)
        key_acc = key_acc.at[flat_ids].add(grad_key.reshape(-1, TILE, head_width))
        value_acc = value_acc.at[flat_ids].add(grad_value.reshape(-1, TILE, head_width))
        return ((key_acc, value_acc), grad_query)
    empty_acc = jnp.zeros((count_tiles, TILE, head_width), jnp.float32)
    (key_acc, value_acc), grad_query = lax.scan(one_group, (empty_acc, empty_acc), (query_tiles, grad_tiles, log_blocks, chosen))

    def restore(tile_rows):
        return jnp.zeros(query_rows.shape, jnp.bfloat16).at[tile_order].set(tile_rows.reshape(-1, head_width).astype(jnp.bfloat16))
    return (restore(grad_query), restore(key_acc), restore(value_acc))

def reference(queries, key_vectors, values, out_weight, cotangent, neighbours, tile_order):
    video_count, token_count, all_width = queries.shape

    def split_heads(tensor):
        return tensor.reshape(video_count, token_count, HEADS, HD).transpose(0, 2, 1, 3).reshape(video_count * HEADS, token_count, HD)

    def join_heads(tensor):
        return tensor.reshape(video_count, HEADS, token_count, HD).transpose(0, 2, 1, 3).reshape(video_count, token_count, all_width)
    query_heads = split_heads(queries)
    key_heads = split_heads(key_vectors)
    value_heads = split_heads(values)
    attended, log_total = lax.map(lambda members: head_forward(members[0], members[1], members[2], tile_order, neighbours), (query_heads, key_heads, value_heads))
    attended_rows = join_heads(attended).reshape(video_count * token_count, all_width)
    cot_rows = cotangent.reshape(video_count * token_count, -1)
    projected = jnp.dot(attended_rows, out_weight, preferred_element_type=jnp.float32).astype(jnp.bfloat16).reshape(video_count, token_count, -1)
    grad_attended = jnp.dot(cot_rows, out_weight.T, preferred_element_type=jnp.float32).astype(jnp.bfloat16)
    grad_weight = jnp.dot(attended_rows.T, cot_rows, preferred_element_type=jnp.float32).astype(jnp.bfloat16)
    grad_heads = split_heads(grad_attended.reshape(video_count, token_count, all_width))
    grad_query, grad_key, grad_value = lax.map(lambda members: head_backward(members[0], members[1], members[2], members[3], members[4], tile_order, neighbours), (query_heads, key_heads, value_heads, grad_heads, log_total))
    return (projected, join_heads(grad_query), join_heads(grad_key), join_heads(grad_value), grad_weight)
```

```python
import math

import jax
import jax.numpy as jnp
import numpy as np
from jax import lax
from jax.experimental import pallas as pl
from jax.experimental.pallas import tpu as pltpu
from jax.sharding import Mesh, PartitionSpec as P

T=192; NT=18; NB=9; N=T*NT; KC=T*NB; HD=128
bf=jnp.bfloat16; f32=jnp.float32
SC=1.0/math.sqrt(HD); LOG2E=math.log2(math.e)
PITCH=4

def permute_rows(order_ref, src, dst, width, scatter, unroll=16):
    def body(i, c):
        for u in range(unroll):
            p=i*unroll+u
            t=order_ref[p]
            a,b=(t,p) if scatter else (p,t)
            dst[pl.ds(a*width,width),:]=src[pl.ds(b*width,width),:]
        return c
    lax.fori_loop(0,N//unroll,body,0)

def k1(order_ref, neigh_ref, qkv_ref, att_ref, qp_ref, kp_ref, vp_ref, o_ref, rinv_ref, e_ref, tok, per, kc, vc, s_ref):
    t=pl.program_id(0)
    @pl.when(t==0)
    def _():
        for j in range(3):
            for s in range(16):
                tok[pl.ds(s*216*PITCH+j,216,stride=PITCH),:]=qkv_ref[s,j].astype(f32)
        permute_rows(order_ref,tok,per,PITCH,False)
        for j,r in enumerate((qp_ref,kp_ref,vp_ref)):
            for u in range(NT):
                r[pl.ds(u*T,T),:]=per[pl.ds(u*T*PITCH+j,T,stride=PITCH),:].astype(bf)
    for j in range(NB):
        n=neigh_ref[t*NB+j]
        off=pl.multiple_of(n*T,T)
        kc[pl.ds(j*T,T),:]=kp_ref[pl.ds(off,T),:]
        vc[pl.ds(j*T,T),:]=vp_ref[pl.ds(off,T),:]
    q=qp_ref[pl.ds(pl.multiple_of(t*T,T),T),:]
    s=lax.dot_general(q,kc[...],(((1,),(1,)),((),())),preferred_element_type=f32)
    m=jnp.max(s,axis=-1,keepdims=True)
    e=jnp.exp2(s*(SC*LOG2E)-m*(SC*LOG2E))
    l=jnp.sum(e,axis=-1,keepdims=True)
    eb=e.astype(bf)
    e_ref[0]=eb
    rinv=1.0/l
    o=jnp.dot(eb,vc[...],preferred_element_type=f32)*rinv
    rinv_ref[...]=jnp.broadcast_to(rinv,(T,HD))
    o_ref[pl.ds(pl.multiple_of(t*T,T),T),:]=o
    @pl.when(t==NT-1)
    def _():
        permute_rows(order_ref,o_ref,tok,1,True)
        for s in range(16):
            att_ref[s]=tok[pl.ds(s*216,216),:].astype(bf)

def run_k1(order, neigh, qkv):
    full=lambda shape: pl.BlockSpec(shape,lambda t,*_:(0,)*len(shape))
    return pl.pallas_call(k1,
      grid_spec=pltpu.PrefetchScalarGridSpec(num_scalar_prefetch=2,grid=(NT,),
        in_specs=[full((16,3,216,HD))],
        out_specs=[full((16,216,HD)),full((N,HD)),full((N,HD)),full((N,HD)),full((N,HD)),
                   pl.BlockSpec((T,HD),lambda t,*_:(t,0)),pl.BlockSpec((1,T,KC),lambda t,*_:(t,0,0))],
        scratch_shapes=[pltpu.VMEM((N*PITCH,HD),f32),pltpu.VMEM((N*PITCH,HD),f32),pltpu.VMEM((KC,HD),bf),pltpu.VMEM((KC,HD),bf),pltpu.VMEM((T,KC),f32)]),
      out_shape=[jax.ShapeDtypeStruct((16,216,HD),bf)]+[jax.ShapeDtypeStruct((N,HD),bf)]*3+[jax.ShapeDtypeStruct((N,HD),f32),jax.ShapeDtypeStruct((N,HD),f32),jax.ShapeDtypeStruct((NT,T,KC),bf)],
      compiler_params=pltpu.CompilerParams(vmem_limit_bytes=60*1024*1024),
      name="attend")(order,neigh,qkv)

def k2(order_ref, neigh_ref, g_ref, qp_ref, kp_ref, vp_ref, o_ref, rinv_ref, e_ref, out_ref, tok, gp, acc, kc, vc):
    t=pl.program_id(0)
    @pl.when(t==0)
    def _():
        for s in range(16):
            tok[pl.ds(s*216,216),:]=g_ref[s].astype(f32)
        permute_rows(order_ref,tok,gp,1,False)
        for u in range(NT*PITCH):
            acc[pl.ds(u*T,T),:]=jnp.zeros((T,HD),f32)
    ns=[]
    for j in range(NB):
        n=neigh_ref[t*NB+j]
        off=pl.multiple_of(n*T,T); ns.append(n)
        kc[pl.ds(j*T,T),:]=kp_ref[pl.ds(off,T),:]
        vc[pl.ds(j*T,T),:]=vp_ref[pl.ds(off,T),:]
    ts=pl.ds(pl.multiple_of(t*T,T),T)
    q=qp_ref[ts,:]
    gs=(gp[ts,:]*rinv_ref[...]).astype(bf)
    d=jnp.sum(gs.astype(f32)*o_ref[ts,:],axis=-1,keepdims=True)
    dp=lax.dot_general(gs,vc[...],(((1,),(1,)),((),())),preferred_element_type=f32)
    eb=e_ref[0]
    ds=(eb.astype(f32)*(dp-d)).astype(bf)
    dq=jnp.dot(ds,kc[...],preferred_element_type=f32)*SC
    acc[pl.ds(t*T*PITCH,T,stride=PITCH),:]=dq
    dk=lax.dot_general(ds,q,(((0,),(0,)),((),())),preferred_element_type=f32)*SC
    dv=lax.dot_general(eb,gs,(((0,),(0,)),((),())),preferred_element_type=f32)
    for j in range(NB):
        base=ns[j]*(T*PITCH)
        i1=pl.ds(base+1,T,stride=PITCH); i2=pl.ds(base+2,T,stride=PITCH)
        acc[i1,:]=acc[i1,:]+dk[j*T:(j+1)*T]
        acc[i2,:]=acc[i2,:]+dv[j*T:(j+1)*T]
    @pl.when(t==NT-1)
    def _():
        permute_rows(order_ref,acc,tok,PITCH,True)
        for s in range(16):
            for j in range(3):
                out_ref[s,j]=tok[pl.ds(s*216*PITCH+j,216,stride=PITCH),:].astype(bf)

def run_k2(order, neigh, g, qp,kp,vp,o,rinv,e):
    full=lambda shape: pl.BlockSpec(shape,lambda t,*_:(0,)*len(shape))
    return pl.pallas_call(k2,
      grid_spec=pltpu.PrefetchScalarGridSpec(num_scalar_prefetch=2,grid=(NT,),
        in_specs=[full((16,216,HD)),full((N,HD)),full((N,HD)),full((N,HD)),full((N,HD)),
                   pl.BlockSpec((T,HD),lambda t,*_:(t,0)),pl.BlockSpec((1,T,KC),lambda t,*_:(t,0,0))],
        out_specs=full((16,3,216,HD)),
        scratch_shapes=[pltpu.VMEM((N*PITCH,HD),f32),pltpu.VMEM((N,HD),f32),pltpu.VMEM((N*PITCH,HD),f32),pltpu.VMEM((KC,HD),bf),pltpu.VMEM((KC,HD),bf)]),
      out_shape=jax.ShapeDtypeStruct((16,3,216,HD),bf),
      compiler_params=pltpu.CompilerParams(vmem_limit_bytes=60*1024*1024),
      name="attend_grad")(order,neigh,g,qp,kp,vp,o,rinv,e)


CHIPS = ("y", "zl")
SEQ = ("y", "zl", "c")
VIDEOS = ("x", "zh")


def shift(value, axis, size, step):
    return lax.ppermute(value, axis, [(i, (i + step) % size) for i in range(size)])


def gather_ring(value, axis, size):
    me = lax.axis_index(axis)
    parts = [value] + [shift(value, axis, size, d) for d in range(1, size)]
    out = jnp.zeros((size,) + value.shape, value.dtype)
    for d, part in enumerate(parts):
        out = lax.dynamic_update_index_in_dim(out, part, (me - d) % size, 0)
    return out


def gather_weight(own):
    w = gather_ring(own, "y", 4)
    w = gather_ring(w, "zl", 2)
    w = gather_ring(w, "zh", 2)
    w = gather_ring(w, "x", 4)
    return w.transpose(3, 2, 0, 1, 4, 5).reshape(1024, 2048)


def scatter_weight(part):
    x, zh = lax.axis_index("x"), lax.axis_index("zh")

    def piece(d):
        return lax.dynamic_index_in_dim(part, (x + d) % 4, 1, keepdims=False)

    far = piece(2).astype(bf)
    up, down = piece(1), piece(3)
    a = shift(far[..., :1024], "x", 4, 1)
    b = shift(far[..., 1024:], "x", 4, -1)
    up_low = shift(up[..., 1024:].astype(bf), "x", 4, 1)
    down_low = shift(down[..., :1024].astype(bf), "x", 4, -1)
    up_high = shift((up[..., :1024] + a.astype(f32)).astype(bf), "x", 4, 1)
    down_high = shift((down[..., 1024:] + b.astype(f32)).astype(bf), "x", 4, -1)
    got = jnp.concatenate(
        [up_high.astype(f32) + down_low.astype(f32), up_low.astype(f32) + down_high.astype(f32)],
        axis=-1,
    )
    rows = piece(0) + got
    mine = lax.dynamic_index_in_dim(rows, zh, 1, keepdims=False)
    other = lax.dynamic_index_in_dim(rows, 1 - zh, 1, keepdims=False)
    rows = mine + shift(other.astype(bf), "zh", 2, 1).astype(f32)
    rows = lax.all_to_all(rows.astype(bf), CHIPS, split_axis=0, concat_axis=0, tiled=True)
    return jnp.sum(rows.astype(f32), axis=0).astype(bf)


def local(queries, key_vectors, values, out_weight, cotangent, neighbours, tile_order):
    core = lax.axis_index("c")
    neigh = neighbours.reshape(-1)

    def by_head(tensor):
        return tensor.reshape(216, 16, HD).transpose(1, 0, 2)

    qkv = jnp.stack([by_head(queries[0]), by_head(key_vectors[0]), by_head(values[0])], axis=1)
    qkv = lax.all_to_all(qkv, SEQ, split_axis=0, concat_axis=0, tiled=True)

    cot = cotangent[0]
    cot_other = shift(cot, "c", 2, 1)
    first = core == 0
    cot_chip = jnp.concatenate(
        [jnp.where(first, cot, cot_other), jnp.where(first, cot_other, cot)], axis=0
    )
    weight = gather_weight(out_weight)
    grad = lax.dot_general(
        cot_chip, weight, (((1,), (1,)), ((), ())), preferred_element_type=f32
    ).astype(bf)
    grad = grad.reshape(432, 8, HD).transpose(1, 0, 2)
    grad = lax.all_to_all(grad, CHIPS, split_axis=0, concat_axis=0, tiled=True)

    att, *saved = run_k1(tile_order, neigh, qkv)
    att = lax.all_to_all(att.reshape(8, 432, HD), CHIPS, split_axis=0, concat_axis=0, tiled=True)
    att = att.transpose(1, 0, 2).reshape(432, 1024)
    grads = run_k2(tile_order, neigh, grad.reshape(16, 216, HD), *saved)
    grads = lax.all_to_all(grads, SEQ, split_axis=0, concat_axis=0, tiled=True)

    partial = jnp.dot(att, weight, preferred_element_type=f32)
    mine = lax.dynamic_slice_in_dim(partial, core * 216, 216, 0)
    other = lax.dynamic_slice_in_dim(partial, (1 - core) * 216, 216, 0)
    projected = (mine + shift(other.astype(bf), "c", 2, 1).astype(f32)).astype(bf)

    weight_part = lax.dot_general(
        att, cot_chip, (((0,), (0,)), ((), ())), preferred_element_type=f32
    )
    grad_weight = scatter_weight(weight_part.reshape(8, 4, 2, 16, 2048))

    def by_token(tensor):
        return tensor.transpose(1, 0, 2).reshape(1, 216, 2048)

    return (
        projected[None],
        by_token(grads[:, 0]),
        by_token(grads[:, 1]),
        by_token(grads[:, 2]),
        grad_weight,
    )


def solution(mesh):
    fine = Mesh(np.asarray(mesh.devices).reshape(4, 2, 2, 4, 2), ("y", "zl", "c", "x", "zh"))
    rows = P(VIDEOS, SEQ, None)
    weight = P(SEQ + VIDEOS, None)
    return jax.shard_map(
        local,
        mesh=fine,
        in_specs=(rows, rows, rows, weight, rows, P(), P()),
        out_specs=(rows, rows, rows, rows, weight),
        check_vma=False,
    )
```

```python
import math

import jax
import jax.numpy as jnp
import numpy as np
from jax import lax
from jax.experimental import pallas as pl
from jax.experimental.pallas import tpu as pltpu
from jax.sharding import Mesh, PartitionSpec as P

T=192; NT=18; NB=9; N=T*NT; KC=T*NB; HD=128
bf=jnp.bfloat16; f32=jnp.float32
SC=1.0/math.sqrt(HD); LOG2E=math.log2(math.e)
PITCH=4
COST=pl.CostEstimate(flops=30*10**9,bytes_accessed=20*10**6,transcendentals=0)

def permute_rows(order_ref, src, dst, width, scatter, unroll=16):
    def body(i, c):
        for u in range(unroll):
            p=i*unroll+u
            t=order_ref[p]
            a,b=(t,p) if scatter else (p,t)
            dst[pl.ds(a*width,width),:]=src[pl.ds(b*width,width),:]
        return c
    lax.fori_loop(0,N//unroll,body,0)

def k1(order_ref, neigh_ref, turn_ref, qkv_ref, att_ref, qp_ref, kp_ref, vp_ref, o_ref, rinv_ref, e_ref, tok, per, kc, vc, s_ref):
    t=pl.program_id(0)
    @pl.when(t==0)
    def _():
        for j in range(3):
            for s in range(16):
                tok[pl.ds(s*216*PITCH+j,216,stride=PITCH),:]=qkv_ref[s,j].astype(f32)
        permute_rows(order_ref,tok,per,PITCH,False)
        for j,r in enumerate((qp_ref,kp_ref,vp_ref)):
            for u in range(NT):
                r[pl.ds(u*T,T),:]=per[pl.ds(u*T*PITCH+j,T,stride=PITCH),:].astype(bf)
    for j in range(NB):
        n=neigh_ref[t*NB+j]
        off=pl.multiple_of(n*T,T)
        kc[pl.ds(j*T,T),:]=kp_ref[pl.ds(off,T),:]
        vc[pl.ds(j*T,T),:]=vp_ref[pl.ds(off,T),:]
    q=qp_ref[pl.ds(pl.multiple_of(t*T,T),T),:]
    s=lax.dot_general(q,kc[...],(((1,),(1,)),((),())),preferred_element_type=f32)
    m=jnp.max(s,axis=-1,keepdims=True)
    e=jnp.exp2(s*(SC*LOG2E)-m*(SC*LOG2E))
    l=jnp.sum(e,axis=-1,keepdims=True)
    eb=e.astype(bf)
    e_ref[0]=eb
    rinv=1.0/l
    o=jnp.dot(eb,vc[...],preferred_element_type=f32)*rinv
    rinv_ref[...]=jnp.broadcast_to(rinv,(T,HD))
    o_ref[pl.ds(pl.multiple_of(t*T,T),T),:]=o
    @pl.when(t==NT-1)
    def _():
        permute_rows(order_ref,o_ref,tok,1,True)
        for s in range(16):
            att_ref[s]=pltpu.roll(tok[pl.ds(s*216,216),:],lax.rem(HD-turn_ref[0],HD),1).astype(bf)

def run_k1(order, neigh, turn, qkv):
    full=lambda shape: pl.BlockSpec(shape,lambda t,*_:(0,)*len(shape))
    return pl.pallas_call(k1,
      grid_spec=pltpu.PrefetchScalarGridSpec(num_scalar_prefetch=3,grid=(NT,),
        in_specs=[full((16,3,216,HD))],
        out_specs=[full((16,216,HD)),full((N,HD)),full((N,HD)),full((N,HD)),full((N,HD)),
                   pl.BlockSpec((T,HD),lambda t,*_:(t,0)),pl.BlockSpec((1,T,KC),lambda t,*_:(t,0,0))],
        scratch_shapes=[pltpu.VMEM((N*PITCH,HD),f32),pltpu.VMEM((N*PITCH,HD),f32),pltpu.VMEM((KC,HD),bf),pltpu.VMEM((KC,HD),bf),pltpu.VMEM((T,KC),f32)]),
      out_shape=[jax.ShapeDtypeStruct((16,216,HD),bf)]+[jax.ShapeDtypeStruct((N,HD),bf)]*3+[jax.ShapeDtypeStruct((N,HD),f32),jax.ShapeDtypeStruct((N,HD),f32),jax.ShapeDtypeStruct((NT,T,KC),bf)],
      compiler_params=pltpu.CompilerParams(vmem_limit_bytes=60*1024*1024),
      cost_estimate=COST,name="attend")(order,neigh,turn,qkv)

def k2(order_ref, neigh_ref, turn_ref, g_ref, qp_ref, kp_ref, vp_ref, o_ref, rinv_ref, e_ref, out_ref, tok, gp, acc, kc, vc):
    t=pl.program_id(0)
    @pl.when(t==0)
    def _():
        for s in range(16):
            tok[pl.ds(s*216,216),:]=pltpu.roll(g_ref[s].astype(f32),turn_ref[0],1)
        permute_rows(order_ref,tok,gp,1,False)
        for u in range(NT*PITCH):
            acc[pl.ds(u*T,T),:]=jnp.zeros((T,HD),f32)
    ns=[]
    for j in range(NB):
        n=neigh_ref[t*NB+j]
        off=pl.multiple_of(n*T,T); ns.append(n)
        kc[pl.ds(j*T,T),:]=kp_ref[pl.ds(off,T),:]
        vc[pl.ds(j*T,T),:]=vp_ref[pl.ds(off,T),:]
    ts=pl.ds(pl.multiple_of(t*T,T),T)
    q=qp_ref[ts,:]
    gs=(gp[ts,:]*rinv_ref[...]).astype(bf)
    d=jnp.sum(gs.astype(f32)*o_ref[ts,:],axis=-1,keepdims=True)
    dp=lax.dot_general(gs,vc[...],(((1,),(1,)),((),())),preferred_element_type=f32)
    eb=e_ref[0]
    ds=(eb.astype(f32)*(dp-d)).astype(bf)
    dq=jnp.dot(ds,kc[...],preferred_element_type=f32)*SC
    acc[pl.ds(t*T*PITCH,T,stride=PITCH),:]=dq
    dk=lax.dot_general(ds,q,(((0,),(0,)),((),())),preferred_element_type=f32)*SC
    dv=lax.dot_general(eb,gs,(((0,),(0,)),((),())),preferred_element_type=f32)
    for j in range(NB):
        base=ns[j]*(T*PITCH)
        i1=pl.ds(base+1,T,stride=PITCH); i2=pl.ds(base+2,T,stride=PITCH)
        acc[i1,:]=acc[i1,:]+dk[j*T:(j+1)*T]
        acc[i2,:]=acc[i2,:]+dv[j*T:(j+1)*T]
    @pl.when(t==NT-1)
    def _():
        permute_rows(order_ref,acc,tok,PITCH,True)
        for s in range(16):
            for j in range(3):
                out_ref[s,j]=tok[pl.ds(s*216*PITCH+j,216,stride=PITCH),:].astype(bf)

def run_k2(order, neigh, turn, g, qp,kp,vp,o,rinv,e):
    full=lambda shape: pl.BlockSpec(shape,lambda t,*_:(0,)*len(shape))
    return pl.pallas_call(k2,
      grid_spec=pltpu.PrefetchScalarGridSpec(num_scalar_prefetch=3,grid=(NT,),
        in_specs=[full((16,216,HD)),full((N,HD)),full((N,HD)),full((N,HD)),full((N,HD)),
                   pl.BlockSpec((T,HD),lambda t,*_:(t,0)),pl.BlockSpec((1,T,KC),lambda t,*_:(t,0,0))],
        out_specs=full((16,3,216,HD)),
        scratch_shapes=[pltpu.VMEM((N*PITCH,HD),f32),pltpu.VMEM((N,HD),f32),pltpu.VMEM((N*PITCH,HD),f32),pltpu.VMEM((KC,HD),bf),pltpu.VMEM((KC,HD),bf)]),
      out_shape=jax.ShapeDtypeStruct((16,3,216,HD),bf),
      compiler_params=pltpu.CompilerParams(vmem_limit_bytes=60*1024*1024),
      cost_estimate=COST,name="attend_grad")(order,neigh,turn,g,qp,kp,vp,o,rinv,e)


CHIPS = ("y", "zl")
SEQ = ("y", "zl", "c")
VIDEOS = ("x", "zh")


def shift(value, axis, size, step):
    return lax.ppermute(value, axis, [(i, (i + step) % size) for i in range(size)])


def in_place(axis, own, other):
    low = lax.axis_index(axis) == 0
    return jnp.concatenate([jnp.where(low, own, other), jnp.where(low, other, own)], axis=0)


def around(value, axis):
    half = value.shape[0] // 2
    after, before = shift(value, axis, 4, -1), shift(value, axis, 4, 1)
    far = [shift(after[:half], axis, 4, -1), shift(before[half:], axis, 4, 1)]
    return [after, jnp.concatenate(far, axis=0), before]


def gather_weight(own, qkv):
    w = in_place("zh", own, shift(own, "zh", 2, 1))
    w = in_place("zl", w[None], shift(w, "zl", 2, 1)[None])
    y = lax.axis_index("y")
    ring = jnp.stack([w] + around(w, "y"))
    ring = jnp.concatenate([ring, ring], axis=0)
    w = lax.dynamic_slice_in_dim(ring, 4 - y, 4, 0).reshape(8, 32, 2048)
    w, qkv = lax.optimization_barrier((w, qkv))
    return jnp.concatenate([w] + around(w, "x"), axis=1), qkv


def scatter_weight(part, after_this):
    def low(value):
        return value.astype(bf)

    own, after, far, before = (part[:, d] for d in range(4))
    far_up = shift(low(far[:4]), "x", 4, 1)
    far_down = shift(low(far[4:]), "x", 4, -1)
    up_plain = shift(low(after[4:]), "x", 4, 1)
    down_plain = shift(low(before[:4]), "x", 4, -1)
    up_sum = shift(low(after[:4] + far_up.astype(f32)), "x", 4, 1)
    down_sum = shift(low(before[4:] + far_down.astype(f32)), "x", 4, -1)
    got = jnp.concatenate(
        [
            up_sum.astype(f32) + down_plain.astype(f32),
            up_plain.astype(f32) + down_sum.astype(f32),
        ],
        axis=0,
    )
    rows, after_this = lax.optimization_barrier((low(own + got).reshape(16, 16, 2048), after_this))
    rows = lax.all_to_all(rows, ("y", "zl", "zh"), split_axis=0, concat_axis=0, tiled=True)
    return low(jnp.sum(rows.astype(f32), axis=0)), after_this


def local(queries, key_vectors, values, out_weight, cotangent, neighbours, tile_order):
    core = lax.axis_index("c")
    turn = (lax.axis_index("x") * 32).astype(jnp.int32).reshape(1)
    neigh = neighbours.reshape(-1)

    def by_head(tensor):
        return tensor.reshape(216, 16, HD).transpose(1, 0, 2)

    qkv = jnp.stack([by_head(queries[0]), by_head(key_vectors[0]), by_head(values[0])], axis=1)
    weight, qkv = gather_weight(out_weight, qkv)
    weight = weight.reshape(1024, 2048)
    qkv = lax.all_to_all(qkv, SEQ, split_axis=0, concat_axis=0, tiled=True)

    cot = cotangent[0]
    cot_other = shift(cot, "c", 2, 1)
    first = core == 0
    cot_chip = jnp.concatenate(
        [jnp.where(first, cot, cot_other), jnp.where(first, cot_other, cot)], axis=0
    )
    grad = lax.dot_general(
        cot_chip, weight, (((1,), (1,)), ((), ())), preferred_element_type=f32
    ).astype(bf)
    grad = grad.reshape(432, 8, HD).transpose(1, 0, 2)
    grad, qkv = lax.optimization_barrier((grad, qkv))
    grad = lax.all_to_all(grad, CHIPS, split_axis=0, concat_axis=0, tiled=True)

    att, *saved = run_k1(tile_order, neigh, turn, qkv)
    att, grad = lax.optimization_barrier((att, grad))
    att = lax.all_to_all(att.reshape(8, 432, HD), CHIPS, split_axis=0, concat_axis=0, tiled=True)
    att = att.transpose(1, 0, 2).reshape(432, 1024)
    grads = run_k2(tile_order, neigh, turn, grad.reshape(16, 216, HD), *saved)
    att, grads = lax.optimization_barrier((att, grads))
    grads = lax.all_to_all(grads, SEQ, split_axis=0, concat_axis=0, tiled=True)

    partial = jnp.dot(att, weight, preferred_element_type=f32)
    mine = lax.dynamic_slice_in_dim(partial, core * 216, 216, 0)
    other = lax.dynamic_slice_in_dim(partial, (1 - core) * 216, 216, 0)
    projected = (mine + shift(other.astype(bf), "c", 2, 1).astype(f32)).astype(bf)

    weight_part = lax.dot_general(
        att, cot_chip, (((0,), (0,)), ((), ())), preferred_element_type=f32
    )
    grad_weight, grads = scatter_weight(weight_part.reshape(8, 4, 32, 2048), grads)

    def by_token(tensor):
        return tensor.transpose(1, 0, 2).reshape(1, 216, 2048)

    return (
        projected[None],
        by_token(grads[:, 0]),
        by_token(grads[:, 1]),
        by_token(grads[:, 2]),
        grad_weight,
    )


def solution(mesh):
    fine = Mesh(np.asarray(mesh.devices).reshape(4, 2, 2, 4, 2), ("y", "zl", "c", "x", "zh"))
    rows = P(VIDEOS, SEQ, None)
    weight = P(SEQ + VIDEOS, None)
    return jax.shard_map(
        local,
        mesh=fine,
        in_specs=(rows, rows, rows, weight, rows, P(), P()),
        out_specs=(rows, rows, rows, rows, weight),
        check_vma=False,
    )
```

```python
import math

import jax
import jax.numpy as jnp
import numpy as np
from jax import lax
from jax.experimental import pallas as pl
from jax.experimental.pallas import tpu as pltpu
from jax.sharding import Mesh, PartitionSpec as P

T=192; NT=18; NB=9; N=T*NT; KC=T*NB; HD=128
bf=jnp.bfloat16; f32=jnp.float32
SC=1.0/math.sqrt(HD); LOG2E=math.log2(math.e)
PITCH=4
KP=1792; BW=256; BLOCKS=KP//BW
U1=2; U2=2
COST=pl.CostEstimate(flops=30*10**9,bytes_accessed=20*10**6,transcendentals=0)

def permute_rows(order_ref, src, dst, width, scatter, unroll=32):
    def body(i, c):
        for u in range(unroll):
            p=i*unroll+u
            t=order_ref[p]
            a,b=(t,p) if scatter else (p,t)
            dst[pl.ds(a*width,width),:]=src[pl.ds(b*width,width),:]
        return c
    lax.fori_loop(0,N//unroll,body,0)

def load_keys(t, to, rows, neigh_ref):
    for j in range(NB):
        to[pl.ds(j*T,T),:]=rows[pl.ds(pl.multiple_of(neigh_ref[t*NB+j]*T,T),T),:]

def scores_ready(t, qp_ref, kp_ref, kc, neigh_ref):
    load_keys(t,kc,kp_ref,neigh_ref)
    kc[pl.ds(KC,KP-KC),:]=kc[pl.ds(KC-(KP-KC),KP-KC),:]
    return qp_ref[pl.ds(pl.multiple_of(t*T,T),T),:]

def k1(order_ref, neigh_ref, turn_ref, qkv_ref, att_ref, qp_ref, kp_ref, vp_ref, o_ref, rinv_ref, e_ref, tok, per, kc, vc, held, sb, mx):
    i=pl.program_id(0)
    R=U1*T
    @pl.when(i==0)
    def _():
        for j in range(3):
            for s in range(16):
                tok[pl.ds(s*216*PITCH+j,216,stride=PITCH),:]=qkv_ref[s,j].astype(f32)
        permute_rows(order_ref,tok,per,PITCH,False)
        for j,r in enumerate((qp_ref,kp_ref,vp_ref)):
            for u in range(NT):
                r[pl.ds(u*T,T),:]=per[pl.ds(u*T*PITCH+j,T,stride=PITCH),:].astype(bf)
        vc[pl.ds(KC,KP-KC),:]=jnp.zeros((KP-KC,HD),bf)
        q=scores_ready(0,qp_ref,kp_ref,kc,neigh_ref)
        s=lax.dot_general(q,kc[...],(((1,),(1,)),((),())),preferred_element_type=f32)
        sb[0]=s
        top=s[:,:HD]
        for b in range(1,KP//HD):
            top=jnp.maximum(top,s[:,b*HD:(b+1)*HD])
        mx[0]=top
    back=jnp.maximum(i-1,0)*R
    for p in range(R):
        tok[pl.ds(order_ref[back+p],1),:]=held[pl.ds(p,1),:]
    for u in range(2):
        t=2*i+u
        load_keys(t,vc,vp_ref,neigh_ref)
        nq=scores_ready(jnp.minimum(t+1,NT-1),qp_ref,kp_ref,kc,neigh_ref)
        mc=jnp.max(mx[u],axis=-1,keepdims=True)*(SC*LOG2E)
        total=jnp.zeros((T,HD),f32)
        o=jnp.zeros((T,HD),f32)
        top=None
        for b in range(BLOCKS):
            cols=pl.ds(b*BW,BW)
            s=lax.dot_general(nq,kc[cols,:],(((1,),(1,)),((),())),preferred_element_type=f32)
            sb[1-u,:,cols]=s
            part=jnp.maximum(s[:,:HD],s[:,HD:])
            top=part if top is None else jnp.maximum(top,part)
            e=jnp.exp2(sb[u,:,cols]*(SC*LOG2E)-mc)
            right=e[:,HD:]
            if b==BLOCKS-1:
                right=jnp.where(lax.broadcasted_iota(jnp.int32,(T,HD),1)<KC%HD,right,0.0)
            total=total+(e[:,:HD]+right)
            eb=e.astype(bf)
            e_ref[u,:,cols]=eb
            o=o+jnp.dot(eb,vc[cols,:],preferred_element_type=f32)
        mx[1-u]=top
        rinv=1.0/jnp.sum(total,axis=-1,keepdims=True)
        o=o*rinv
        rinv_ref[pl.ds(u*T,T),:]=jnp.broadcast_to(rinv,(T,HD))
        o_ref[pl.ds(u*T,T),:]=o
        held[pl.ds(u*T,T),:]=o
    @pl.when(i==NT//U1-1)
    def _():
        def last(c,_):
            for w in range(32):
                p=c*32+w
                tok[pl.ds(order_ref[N-R+p],1),:]=held[pl.ds(p,1),:]
            return _
        lax.fori_loop(0,R//32,last,0)
        for s in range(16):
            att_ref[s]=pltpu.roll(tok[pl.ds(s*216,216),:],lax.rem(HD-turn_ref[0],HD),1).astype(bf)

def run_k1(order, neigh, turn, qkv):
    full=lambda shape: pl.BlockSpec(shape,lambda t,*_:(0,)*len(shape))
    return pl.pallas_call(k1,
      grid_spec=pltpu.PrefetchScalarGridSpec(num_scalar_prefetch=3,grid=(NT//U1,),
        in_specs=[full((16,3,216,HD))],
        out_specs=[full((16,216,HD)),full((N,HD)),full((N,HD)),full((N,HD)),pl.BlockSpec((U1*T,HD),lambda t,*_:(t,0)),
                   pl.BlockSpec((U1*T,HD),lambda t,*_:(t,0)),pl.BlockSpec((U1,T,KP),lambda t,*_:(t,0,0))],
        scratch_shapes=[pltpu.VMEM((N*PITCH,HD),f32),pltpu.VMEM((N*PITCH,HD),f32),pltpu.VMEM((KP,HD),bf),pltpu.VMEM((KP,HD),bf),pltpu.VMEM((U1*T,HD),f32),pltpu.VMEM((2,T,KP),f32),pltpu.VMEM((2,T,HD),f32)]),
      out_shape=[jax.ShapeDtypeStruct((16,216,HD),bf)]+[jax.ShapeDtypeStruct((N,HD),bf)]*3+[jax.ShapeDtypeStruct((N,HD),f32),jax.ShapeDtypeStruct((N,HD),f32),jax.ShapeDtypeStruct((NT,T,KP),bf)],
      compiler_params=pltpu.CompilerParams(vmem_limit_bytes=60*1024*1024),
      cost_estimate=COST,name="attend")(order,neigh,turn,qkv)

def k2(order_ref, neigh_ref, turn_ref, g_ref, qp_ref, kp_ref, vp_ref, o_ref, rinv_ref, e_ref, out_ref, tok, gp, acc, kc, vc):
    i=pl.program_id(0)
    R=U2*T
    @pl.when(i==0)
    def _():
        for s in range(16):
            tok[pl.ds(s*216,216),:]=pltpu.roll(g_ref[s].astype(f32),turn_ref[0],1)
        def first(c,_):
            for w in range(32):
                p=c*32+w
                gp[pl.ds(p,1),:]=tok[pl.ds(order_ref[p],1),:]
            return _
        lax.fori_loop(0,R//32,first,0)
        for u in range(NT*PITCH):
            acc[pl.ds(u*T,T),:]=jnp.zeros((T,HD),f32)
    g=gp[...]
    ahead=jnp.minimum((i+1)*R,N-R)
    for p in range(R):
        gp[pl.ds(p,1),:]=tok[pl.ds(order_ref[ahead+p],1),:]
    gs_all=(g*rinv_ref[...]).astype(bf)
    d_all=jnp.sum(gs_all.astype(f32)*o_ref[...],axis=-1,keepdims=True)
    for u in range(U2):
        t=i*U2+u
        ns=[]
        for j in range(NB):
            n=neigh_ref[t*NB+j]
            off=pl.multiple_of(n*T,T); ns.append(n)
            kc[u,pl.ds(j*T,T),:]=kp_ref[pl.ds(off,T),:]
            vc[u,pl.ds(j*T,T),:]=vp_ref[pl.ds(off,T),:]
        q=qp_ref[pl.ds(u*T,T),:]
        gs=gs_all[u*T:(u+1)*T]
        d=d_all[u*T:(u+1)*T]
        dp=lax.dot_general(gs,vc[u],(((1,),(1,)),((),())),preferred_element_type=f32)
        eb=e_ref[u,:,:KC]
        ds=(eb.astype(f32)*(dp-d)).astype(bf)
        dq=jnp.dot(ds,kc[u],preferred_element_type=f32)
        acc[pl.ds(t*T*PITCH,T,stride=PITCH),:]=dq
        dk=lax.dot_general(ds,q,(((0,),(0,)),((),())),preferred_element_type=f32)
        dv=lax.dot_general(eb,gs,(((0,),(0,)),((),())),preferred_element_type=f32)
        for j in range(NB):
            base=ns[j]*(T*PITCH)
            i1=pl.ds(base+1,T,stride=PITCH); i2=pl.ds(base+2,T,stride=PITCH)
            acc[i1,:]=acc[i1,:]+dk[j*T:(j+1)*T]
            acc[i2,:]=acc[i2,:]+dv[j*T:(j+1)*T]
    @pl.when(i==NT//U2-1)
    def _():
        permute_rows(order_ref,acc,tok,PITCH,True)
        for s in range(16):
            for j in range(3):
                rows=tok[pl.ds(s*216*PITCH+j,216,stride=PITCH),:]
                out_ref[s,j]=(rows*SC if j<2 else rows).astype(bf)

def run_k2(order, neigh, turn, g, qp,kp,vp,o,rinv,e):
    full=lambda shape: pl.BlockSpec(shape,lambda t,*_:(0,)*len(shape))
    row=pl.BlockSpec((U2*T,HD),lambda t,*_:(t,0))
    return pl.pallas_call(k2,
      grid_spec=pltpu.PrefetchScalarGridSpec(num_scalar_prefetch=3,grid=(NT//U2,),
        in_specs=[full((16,216,HD)),row,full((N,HD)),full((N,HD)),row,
                   row,pl.BlockSpec((U2,T,KP),lambda t,*_:(t,0,0))],
        out_specs=full((16,3,216,HD)),
        scratch_shapes=[pltpu.VMEM((N*PITCH,HD),f32),pltpu.VMEM((U2*T,HD),f32),pltpu.VMEM((N*PITCH,HD),f32),pltpu.VMEM((U2,KC,HD),bf),pltpu.VMEM((U2,KC,HD),bf)]),
      out_shape=jax.ShapeDtypeStruct((16,3,216,HD),bf),
      compiler_params=pltpu.CompilerParams(vmem_limit_bytes=60*1024*1024),
      cost_estimate=COST,name="attend_grad")(order,neigh,turn,g,qp,kp,vp,o,rinv,e)


def rows_kernel(y_ref, cot_ref, near, near_after, low_half, high_half, near_before, far, far_after, far_before, grad_ref, w_ref):
    cot = cot_ref[...]
    for r in range(4):
        for zl in range(2):
            at = {0: 0, 1: 2, 3: 4}.get(r, 0) + zl
            if r == 2:
                opposite = high_half[3] if zl else low_half[3]
                parts = [far[zl], far_after[zl], opposite, far_before[zl]]
            else:
                opposite = low_half[at] if at < 3 else high_half[at - 3]
                parts = [near[at], near_after[at], opposite, near_before[at]]
            head = lax.rem(y_ref[0] + r, 4) * 2 + zl
            for d in range(4):
                w_ref[head, pl.ds(d * 32, 32), :] = parts[d]
            grad_ref[head] = lax.dot_general(
                cot, w_ref[head], (((1,), (1,)), ((), ())), preferred_element_type=f32
            ).astype(bf)


def run_rows(y, cot, near, far):
    whole = pl.BlockSpec(memory_space=pltpu.VMEM)
    return pl.pallas_call(
        rows_kernel,
        in_specs=[pl.BlockSpec(memory_space=pltpu.SMEM)] + [whole] * 9,
        out_specs=[whole, whole],
        out_shape=[
            jax.ShapeDtypeStruct((8, 432, HD), bf),
            jax.ShapeDtypeStruct((8, HD, 2048), bf),
        ],
        compiler_params=pltpu.CompilerParams(vmem_limit_bytes=40 * 1024 * 1024),
        cost_estimate=pl.CostEstimate(flops=5 * 10**9, bytes_accessed=10**7, transcendentals=0),
        name="grad_rows",
    )(y, cot, *near, *far)


CHIPS = ("y", "zl")
SEQ = ("y", "zl", "c")
VIDEOS = ("x", "zh")


def shift(value, axis, size, step):
    return lax.ppermute(value, axis, [(i, (i + step) % size) for i in range(size)])


def in_place(axis, own, other):
    low = lax.axis_index(axis) == 0
    return jnp.concatenate([jnp.where(low, own, other), jnp.where(low, other, own)], axis=0)


def around(value, axis):
    half = value.shape[0] // 2
    after, before = shift(value, axis, 4, -1), shift(value, axis, 4, 1)
    far = [shift(after[:half], axis, 4, -1), shift(before[half:], axis, 4, 1)]
    return [after, jnp.concatenate(far, axis=0), before]


def gather_weight(own, qkv):
    pairs = [[(i, i ^ flip) for i in range(4)] for flip in (1, 2, 3)]
    next_zh, next_zl, next_both = (lax.ppermute(own, ("zl", "zh"), pair) for pair in pairs)
    w = in_place("zl", in_place("zh", own, next_zh)[None], in_place("zh", next_zl, next_both)[None])
    y = lax.axis_index("y")
    ring = jnp.stack([w] + around(w, "y"))
    ring = jnp.concatenate([ring, ring], axis=0)
    w = lax.dynamic_slice_in_dim(ring, 4 - y, 4, 0).reshape(8, 32, 2048)
    w, qkv = lax.optimization_barrier((w, qkv))
    return jnp.concatenate([w] + around(w, "x"), axis=1), qkv


def low(value):
    return value.astype(bf)


def sum_last(rows, grads):
    def at(value, index):
        return lax.dynamic_index_in_dim(value, index, 0, keepdims=False)

    y, z = lax.axis_index("y"), lax.axis_index(("zl", "zh"))
    rows = rows.reshape(4, 4, 16, 2048)
    got = [shift(at(rows, (y + d) % 4), "y", 4, d) for d in (1, 2, 3)]
    *got, grads = lax.optimization_barrier((*got, grads))
    rows = low(sum((part.astype(f32) for part in got), at(rows, y).astype(f32)))
    total = at(rows, z).astype(f32)
    for flip in (1, 2, 3):
        pairs = [(i, i ^ flip) for i in range(4)]
        total = total + lax.ppermute(at(rows, z ^ flip), ("zl", "zh"), pairs).astype(f32)
    return low(total), grads


def local(queries, key_vectors, values, out_weight, cotangent, neighbours, tile_order):
    core = lax.axis_index("c")
    turn = (lax.axis_index("x") * 32).astype(jnp.int32).reshape(1)
    neigh = neighbours.reshape(-1)

    def by_head(tensor):
        return tensor.reshape(216, 16, HD).transpose(1, 0, 2)

    qkv = jnp.stack([by_head(queries[0]), by_head(key_vectors[0]), by_head(values[0])], axis=1)
    cot = cotangent[0]
    weight, qkv = gather_weight(out_weight, qkv)
    weight = weight.reshape(1024, 2048)
    qkv = lax.all_to_all(qkv, SEQ, split_axis=0, concat_axis=0, tiled=True)

    def of_chip(mine, theirs=None):
        theirs = shift(mine, "c", 2, 1) if theirs is None else theirs
        return jnp.concatenate(
            [jnp.where(core == 0, mine, theirs), jnp.where(core == 0, theirs, mine)], axis=0
        )

    cot_chip = of_chip(cot)
    grad = lax.dot_general(
        cot_chip, weight, (((1,), (1,)), ((), ())), preferred_element_type=f32
    ).astype(bf)
    grad = grad.reshape(432, 8, HD).transpose(1, 0, 2)
    grad, qkv = lax.optimization_barrier((grad, qkv))
    grad = lax.all_to_all(grad, CHIPS, split_axis=0, concat_axis=0, tiled=True)

    att, *saved = run_k1(tile_order, neigh, turn, qkv)
    att, grad, cot = lax.optimization_barrier((att, grad, cot))
    cots = [shift(cot, "x", 4, d) for d in (1, 2, 3)]
    att = lax.all_to_all(att.reshape(8, 432, HD), CHIPS, split_axis=0, concat_axis=0, tiled=True)
    att = att.transpose(1, 0, 2).reshape(432, 1024)
    grads = run_k2(tile_order, neigh, turn, grad.reshape(16, 216, HD), *saved)
    att, grads, *cots = lax.optimization_barrier((att, grads, *cots))
    grads = lax.all_to_all(grads, SEQ, split_axis=0, concat_axis=0, tiled=True)

    first_other = shift(cots[0], "c", 2, 1)
    att, first_other = lax.optimization_barrier((att, first_other))
    shares = att.reshape(432, 8, 4, 32).transpose(2, 0, 1, 3).reshape(4, 432, 256)
    shares = [shares[0]] + [shift(shares[d], "x", 4, d) for d in (1, 2, 3)]
    rows = jnp.zeros((256, 2048), f32)
    for share, rows_of in zip(shares, [cot_chip, of_chip(cots[0], first_other), of_chip(cots[1]), of_chip(cots[2])]):
        rows = rows + lax.dot_general(
            share, rows_of, (((0,), (0,)), ((), ())), preferred_element_type=f32
        )
    rows = low(rows).reshape(16, 16, 2048)
    partial = jnp.dot(att, weight, preferred_element_type=f32)
    mine = lax.dynamic_slice_in_dim(partial, core * 216, 216, 0)
    other = lax.dynamic_slice_in_dim(partial, (1 - core) * 216, 216, 0).astype(bf)
    projected = (mine + shift(other, "c", 2, 1).astype(f32)).astype(bf)
    grad_weight, grads = sum_last(rows, grads)

    def by_token(tensor):
        return tensor.transpose(1, 0, 2).reshape(1, 216, 2048)

    return (
        projected[None],
        by_token(grads[:, 0]),
        by_token(grads[:, 1]),
        by_token(grads[:, 2]),
        grad_weight,
    )


def solution(mesh):
    fine = Mesh(np.asarray(mesh.devices).reshape(4, 2, 2, 4, 2), ("y", "zl", "c", "x", "zh"))
    rows = P(VIDEOS, SEQ, None)
    weight = P(SEQ + VIDEOS, None)
    return jax.shard_map(
        local,
        mesh=fine,
        in_specs=(rows, rows, rows, weight, rows, P(), P()),
        out_specs=(rows, rows, rows, rows, weight),
        check_vma=False,
    )
```

```python
import math

import jax
import jax.numpy as jnp
import numpy as np
from jax import lax
from jax.experimental import pallas as pl
from jax.experimental.pallas import tpu as pltpu
from jax.sharding import Mesh, PartitionSpec as P

T=192; NT=18; NB=9; N=T*NT; KC=T*NB; HD=128
bf=jnp.bfloat16; f32=jnp.float32
SC=1.0/math.sqrt(HD); LOG2E=math.log2(math.e)
PITCH=4
KP=1792; BW=256; BLOCKS=KP//BW
U1=2; U2=2
COST=pl.CostEstimate(flops=30*10**9,bytes_accessed=20*10**6,transcendentals=0)

def permute_rows(order_ref, src, dst, width, scatter, unroll=32):
    def body(i, c):
        for u in range(unroll):
            p=i*unroll+u
            t=order_ref[p]
            a,b=(t,p) if scatter else (p,t)
            dst[pl.ds(a*width,width),:]=src[pl.ds(b*width,width),:]
        return c
    lax.fori_loop(0,N//unroll,body,0)

def load_keys(t, to, rows, neigh_ref):
    for j in range(NB):
        to[pl.ds(j*T,T),:]=rows[pl.ds(pl.multiple_of(neigh_ref[t*NB+j]*T,T),T),:]

def scores_ready(t, qp_ref, kp_ref, kc, neigh_ref):
    load_keys(t,kc,kp_ref,neigh_ref)
    kc[pl.ds(KC,KP-KC),:]=kc[pl.ds(KC-(KP-KC),KP-KC),:]
    return qp_ref[pl.ds(pl.multiple_of(t*T,T),T),:]

def k1(order_ref, neigh_ref, turn_ref, qkv_ref, att_ref, qp_ref, kp_ref, vp_ref, o_ref, rinv_ref, e_ref, tok, per, kc, vc, held, sb, mx):
    i=pl.program_id(0)
    R=U1*T
    @pl.when(i==0)
    def _():
        for j in range(3):
            for s in range(16):
                tok[pl.ds(s*216*PITCH+j,216,stride=PITCH),:]=qkv_ref[s,j].astype(f32)
        permute_rows(order_ref,tok,per,PITCH,False)
        for j,r in enumerate((qp_ref,kp_ref,vp_ref)):
            for u in range(NT):
                r[pl.ds(u*T,T),:]=per[pl.ds(u*T*PITCH+j,T,stride=PITCH),:].astype(bf)
        vc[pl.ds(KC,KP-KC),:]=jnp.zeros((KP-KC,HD),bf)
        q=scores_ready(0,qp_ref,kp_ref,kc,neigh_ref)
        s=lax.dot_general(q,kc[...],(((1,),(1,)),((),())),preferred_element_type=f32)
        sb[0]=s
        top=s[:,:HD]
        for b in range(1,KP//HD):
            top=jnp.maximum(top,s[:,b*HD:(b+1)*HD])
        mx[0]=top
    back=jnp.maximum(i-1,0)*R
    for p in range(R):
        tok[pl.ds(order_ref[back+p],1),:]=held[pl.ds(p,1),:]
    for u in range(2):
        t=2*i+u
        load_keys(t,vc,vp_ref,neigh_ref)
        nq=scores_ready(jnp.minimum(t+1,NT-1),qp_ref,kp_ref,kc,neigh_ref)
        mc=jnp.max(mx[u],axis=-1,keepdims=True)*(SC*LOG2E)
        total=jnp.zeros((T,HD),f32)
        o=jnp.zeros((T,HD),f32)
        top=None
        for b in range(BLOCKS):
            cols=pl.ds(b*BW,BW)
            s=lax.dot_general(nq,kc[cols,:],(((1,),(1,)),((),())),preferred_element_type=f32)
            sb[1-u,:,cols]=s
            part=jnp.maximum(s[:,:HD],s[:,HD:])
            top=part if top is None else jnp.maximum(top,part)
            e=jnp.exp2(sb[u,:,cols]*(SC*LOG2E)-mc)
            right=e[:,HD:]
            if b==BLOCKS-1:
                right=jnp.where(lax.broadcasted_iota(jnp.int32,(T,HD),1)<KC%HD,right,0.0)
            total=total+(e[:,:HD]+right)
            eb=e.astype(bf)
            e_ref[u,:,cols]=eb
            o=o+jnp.dot(eb,vc[cols,:],preferred_element_type=f32)
        mx[1-u]=top
        rinv=1.0/jnp.sum(total,axis=-1,keepdims=True)
        o=o*rinv
        rinv_ref[pl.ds(u*T,T),:]=jnp.broadcast_to(rinv,(T,HD))
        o_ref[pl.ds(u*T,T),:]=o
        held[pl.ds(u*T,T),:]=o
    @pl.when(i==NT//U1-1)
    def _():
        def last(c,_):
            for w in range(32):
                p=c*32+w
                tok[pl.ds(order_ref[N-R+p],1),:]=held[pl.ds(p,1),:]
            return _
        lax.fori_loop(0,R//32,last,0)
        for s in range(16):
            att_ref[s]=pltpu.roll(tok[pl.ds(s*216,216),:],lax.rem(HD-turn_ref[0],HD),1).astype(bf)

def run_k1(order, neigh, turn, qkv):
    full=lambda shape: pl.BlockSpec(shape,lambda t,*_:(0,)*len(shape))
    return pl.pallas_call(k1,
      grid_spec=pltpu.PrefetchScalarGridSpec(num_scalar_prefetch=3,grid=(NT//U1,),
        in_specs=[full((16,3,216,HD))],
        out_specs=[full((16,216,HD)),full((N,HD)),full((N,HD)),full((N,HD)),pl.BlockSpec((U1*T,HD),lambda t,*_:(t,0)),
                   pl.BlockSpec((U1*T,HD),lambda t,*_:(t,0)),pl.BlockSpec((U1,T,KP),lambda t,*_:(t,0,0))],
        scratch_shapes=[pltpu.VMEM((N*PITCH,HD),f32),pltpu.VMEM((N*PITCH,HD),f32),pltpu.VMEM((KP,HD),bf),pltpu.VMEM((KP,HD),bf),pltpu.VMEM((U1*T,HD),f32),pltpu.VMEM((2,T,KP),f32),pltpu.VMEM((2,T,HD),f32)]),
      out_shape=[jax.ShapeDtypeStruct((16,216,HD),bf)]+[jax.ShapeDtypeStruct((N,HD),bf)]*3+[jax.ShapeDtypeStruct((N,HD),f32),jax.ShapeDtypeStruct((N,HD),f32),jax.ShapeDtypeStruct((NT,T,KP),bf)],
      compiler_params=pltpu.CompilerParams(vmem_limit_bytes=60*1024*1024),
      cost_estimate=COST,name="attend")(order,neigh,turn,qkv)

def k2(order_ref, neigh_ref, turn_ref, g_ref, qp_ref, kp_ref, vp_ref, o_ref, rinv_ref, e_ref, out_ref, tok, gp, acc, kc, vc):
    i=pl.program_id(0)
    R=U2*T
    @pl.when(i==0)
    def _():
        for s in range(16):
            tok[pl.ds(s*216,216),:]=pltpu.roll(g_ref[s].astype(f32),turn_ref[0],1)
        def first(c,_):
            for w in range(32):
                p=c*32+w
                gp[pl.ds(p,1),:]=tok[pl.ds(order_ref[p],1),:]
            return _
        lax.fori_loop(0,R//32,first,0)
        for u in range(NT*PITCH):
            acc[pl.ds(u*T,T),:]=jnp.zeros((T,HD),f32)
    g=gp[...]
    ahead=jnp.minimum((i+1)*R,N-R)
    for p in range(R):
        gp[pl.ds(p,1),:]=tok[pl.ds(order_ref[ahead+p],1),:]
    gs_all=(g*rinv_ref[...]).astype(bf)
    d_all=jnp.sum(gs_all.astype(f32)*o_ref[...],axis=-1,keepdims=True)
    for u in range(U2):
        t=i*U2+u
        ns=[]
        for j in range(NB):
            n=neigh_ref[t*NB+j]
            off=pl.multiple_of(n*T,T); ns.append(n)
            kc[u,pl.ds(j*T,T),:]=kp_ref[pl.ds(off,T),:]
            vc[u,pl.ds(j*T,T),:]=vp_ref[pl.ds(off,T),:]
        q=qp_ref[pl.ds(u*T,T),:]
        gs=gs_all[u*T:(u+1)*T]
        d=d_all[u*T:(u+1)*T]
        dp=lax.dot_general(gs,vc[u],(((1,),(1,)),((),())),preferred_element_type=f32)
        eb=e_ref[u,:,:KC]
        ds=(eb.astype(f32)*(dp-d)).astype(bf)
        dq=jnp.dot(ds,kc[u],preferred_element_type=f32)
        acc[pl.ds(t*T*PITCH,T,stride=PITCH),:]=dq
        dk=lax.dot_general(ds,q,(((0,),(0,)),((),())),preferred_element_type=f32)
        dv=lax.dot_general(eb,gs,(((0,),(0,)),((),())),preferred_element_type=f32)
        for j in range(NB):
            base=ns[j]*(T*PITCH)
            i1=pl.ds(base+1,T,stride=PITCH); i2=pl.ds(base+2,T,stride=PITCH)
            acc[i1,:]=acc[i1,:]+dk[j*T:(j+1)*T]
            acc[i2,:]=acc[i2,:]+dv[j*T:(j+1)*T]
    @pl.when(i==NT//U2-1)
    def _():
        permute_rows(order_ref,acc,tok,PITCH,True)
        for s in range(16):
            for j in range(3):
                rows=tok[pl.ds(s*216*PITCH+j,216,stride=PITCH),:]
                out_ref[s,j]=(rows*SC if j<2 else rows).astype(bf)

def run_k2(order, neigh, turn, g, qp,kp,vp,o,rinv,e):
    full=lambda shape: pl.BlockSpec(shape,lambda t,*_:(0,)*len(shape))
    row=pl.BlockSpec((U2*T,HD),lambda t,*_:(t,0))
    return pl.pallas_call(k2,
      grid_spec=pltpu.PrefetchScalarGridSpec(num_scalar_prefetch=3,grid=(NT//U2,),
        in_specs=[full((16,216,HD)),row,full((N,HD)),full((N,HD)),row,
                   row,pl.BlockSpec((U2,T,KP),lambda t,*_:(t,0,0))],
        out_specs=full((16,3,216,HD)),
        scratch_shapes=[pltpu.VMEM((N*PITCH,HD),f32),pltpu.VMEM((U2*T,HD),f32),pltpu.VMEM((N*PITCH,HD),f32),pltpu.VMEM((U2,KC,HD),bf),pltpu.VMEM((U2,KC,HD),bf)]),
      out_shape=jax.ShapeDtypeStruct((16,3,216,HD),bf),
      compiler_params=pltpu.CompilerParams(vmem_limit_bytes=60*1024*1024),
      cost_estimate=COST,name="attend_grad")(order,neigh,turn,g,qp,kp,vp,o,rinv,e)


def rows_kernel(y_ref, cot_ref, near, near_after, low_half, high_half, near_before, far, far_after, far_before, grad_ref, w_ref):
    cot = cot_ref[...]
    for r in range(4):
        for zl in range(2):
            at = {0: 0, 1: 2, 3: 4}.get(r, 0) + zl
            if r == 2:
                opposite = high_half[3] if zl else low_half[3]
                parts = [far[zl], far_after[zl], opposite, far_before[zl]]
            else:
                opposite = low_half[at] if at < 3 else high_half[at - 3]
                parts = [near[at], near_after[at], opposite, near_before[at]]
            head = lax.rem(y_ref[0] + r, 4) * 2 + zl
            for d in range(4):
                w_ref[head, pl.ds(d * 32, 32), :] = parts[d]
            grad_ref[head] = lax.dot_general(
                cot, w_ref[head], (((1,), (1,)), ((), ())), preferred_element_type=f32
            ).astype(bf)


def run_rows(y, cot, near, far):
    whole = pl.BlockSpec(memory_space=pltpu.VMEM)
    return pl.pallas_call(
        rows_kernel,
        in_specs=[pl.BlockSpec(memory_space=pltpu.SMEM)] + [whole] * 9,
        out_specs=[whole, whole],
        out_shape=[
            jax.ShapeDtypeStruct((8, 432, HD), bf),
            jax.ShapeDtypeStruct((8, HD, 2048), bf),
        ],
        compiler_params=pltpu.CompilerParams(vmem_limit_bytes=40 * 1024 * 1024),
        cost_estimate=pl.CostEstimate(flops=5 * 10**9, bytes_accessed=10**7, transcendentals=0),
        name="grad_rows",
    )(y, cot, *near, *far)


CHIPS = ("y", "zl")
SEQ = ("y", "zl", "c")
VIDEOS = ("x", "zh")


def shift(value, axis, size, step):
    return lax.ppermute(value, axis, [(i, (i + step) % size) for i in range(size)])


def in_place(axis, own, other):
    low = lax.axis_index(axis) == 0
    return jnp.concatenate([jnp.where(low, own, other), jnp.where(low, other, own)], axis=0)


def around(value, axis):
    half = value.shape[0] // 2
    after, before = shift(value, axis, 4, -1), shift(value, axis, 4, 1)
    far = [shift(after[:half], axis, 4, -1), shift(before[half:], axis, 4, 1)]
    return [after, jnp.concatenate(far, axis=0), before]


def gather_weight(own, qkv):
    def along_z(value):
        next_zh, next_zl, next_both = (
            lax.ppermute(value, ("zl", "zh"), [(i, i ^ flip) for i in range(4)]) for flip in (1, 2, 3)
        )
        return in_place(
            "zl", in_place("zh", value, next_zh)[None], in_place("zh", next_zl, next_both)[None]
        )

    opposite = shift(own, "y", 4, 2)
    w = along_z(own)
    y = lax.axis_index("y")
    ring = jnp.stack([w, shift(w, "y", 4, -1), along_z(opposite), shift(w, "y", 4, 1)])
    ring = jnp.concatenate([ring, ring], axis=0)
    w = lax.dynamic_slice_in_dim(ring, 4 - y, 4, 0).reshape(8, 32, 2048)
    w, qkv = lax.optimization_barrier((w, qkv))
    return jnp.concatenate([w] + around(w, "x"), axis=1), qkv


def low(value):
    return value.astype(bf)


def sum_last(rows, grads):
    def at(value, index):
        return lax.dynamic_index_in_dim(value, index, 0, keepdims=False)

    y, z = lax.axis_index("y"), lax.axis_index(("zl", "zh"))
    rows = rows.reshape(4, 4, 16, 2048)
    got = [shift(at(rows, (y + d) % 4), "y", 4, d) for d in (1, 2, 3)]
    *got, grads = lax.optimization_barrier((*got, grads))
    rows = low(sum((part.astype(f32) for part in got), at(rows, y).astype(f32)))
    total = at(rows, z).astype(f32)
    for flip in (1, 2, 3):
        pairs = [(i, i ^ flip) for i in range(4)]
        total = total + lax.ppermute(at(rows, z ^ flip), ("zl", "zh"), pairs).astype(f32)
    return low(total), grads


def local(queries, key_vectors, values, out_weight, cotangent, neighbours, tile_order):
    core = lax.axis_index("c")
    turn = (lax.axis_index("x") * 32).astype(jnp.int32).reshape(1)
    neigh = neighbours.reshape(-1)

    def by_head(tensor):
        return tensor.reshape(216, 16, HD).transpose(1, 0, 2)

    qkv = jnp.stack([by_head(queries[0]), by_head(key_vectors[0]), by_head(values[0])], axis=1)
    cot = cotangent[0]
    weight, qkv = gather_weight(out_weight, qkv)
    weight = weight.reshape(1024, 2048)
    qkv = lax.all_to_all(qkv, SEQ, split_axis=0, concat_axis=0, tiled=True)

    def of_chip(mine, theirs=None):
        theirs = shift(mine, "c", 2, 1) if theirs is None else theirs
        return jnp.concatenate(
            [jnp.where(core == 0, mine, theirs), jnp.where(core == 0, theirs, mine)], axis=0
        )

    cot_chip = of_chip(cot)
    grad = lax.dot_general(
        cot_chip, weight, (((1,), (1,)), ((), ())), preferred_element_type=f32
    ).astype(bf)
    grad = grad.reshape(432, 8, HD).transpose(1, 0, 2)
    grad, qkv = lax.optimization_barrier((grad, qkv))
    grad = lax.all_to_all(grad, CHIPS, split_axis=0, concat_axis=0, tiled=True)

    att, *saved = run_k1(tile_order, neigh, turn, qkv)
    att, grad, cot = lax.optimization_barrier((att, grad, cot))
    cots = [shift(cot, "x", 4, d) for d in (1, 2, 3)]
    att = lax.all_to_all(att.reshape(8, 432, HD), CHIPS, split_axis=0, concat_axis=0, tiled=True)
    att = att.transpose(1, 0, 2).reshape(432, 1024)
    grads = run_k2(tile_order, neigh, turn, grad.reshape(16, 216, HD), *saved)
    att, grads, *cots = lax.optimization_barrier((att, grads, *cots))
    grads = lax.all_to_all(grads, SEQ, split_axis=0, concat_axis=0, tiled=True)

    first_other = shift(cots[0], "c", 2, 1)
    att, first_other = lax.optimization_barrier((att, first_other))
    shares = att.reshape(432, 8, 4, 32).transpose(2, 0, 1, 3).reshape(4, 432, 256)
    shares = [shares[0]] + [shift(shares[d], "x", 4, d) for d in (1, 2, 3)]
    rows = jnp.zeros((256, 2048), f32)
    for share, rows_of in zip(shares, [cot_chip, of_chip(cots[0], first_other), of_chip(cots[1]), of_chip(cots[2])]):
        rows = rows + lax.dot_general(
            share, rows_of, (((0,), (0,)), ((), ())), preferred_element_type=f32
        )
    rows = low(rows).reshape(16, 16, 2048)
    partial = jnp.dot(att, weight, preferred_element_type=f32)
    mine = lax.dynamic_slice_in_dim(partial, core * 216, 216, 0)
    other = lax.dynamic_slice_in_dim(partial, (1 - core) * 216, 216, 0).astype(bf)
    projected = (mine + shift(other, "c", 2, 1).astype(f32)).astype(bf)
    grad_weight, grads = sum_last(rows, grads)

    def by_token(tensor):
        return tensor.transpose(1, 0, 2).reshape(1, 216, 2048)

    return (
        projected[None],
        by_token(grads[:, 0]),
        by_token(grads[:, 1]),
        by_token(grads[:, 2]),
        grad_weight,
    )


def solution(mesh):
    fine = Mesh(np.asarray(mesh.devices).reshape(4, 2, 2, 4, 2), ("y", "zl", "c", "x", "zh"))
    rows = P(VIDEOS, SEQ, None)
    weight = P(SEQ + VIDEOS, None)
    return jax.shard_map(
        local,
        mesh=fine,
        in_specs=(rows, rows, rows, weight, rows, P(), P()),
        out_specs=(rows, rows, rows, rows, weight),
        check_vma=False,
    )
```

```python
import math

import jax
import jax.numpy as jnp
import numpy as np
from jax import lax
from jax.experimental import pallas as pl
from jax.experimental.pallas import tpu as pltpu
from jax.sharding import Mesh, PartitionSpec as P

T=192; NT=18; NB=9; N=T*NT; KC=T*NB; HD=128
bf=jnp.bfloat16; f32=jnp.float32
SC=1.0/math.sqrt(HD); LOG2E=math.log2(math.e)
PITCH=4
PITCH1=3
SPARE=16
KP=1792; BW=256; BLOCKS=KP//BW
U1=2; U2=2
COST=pl.CostEstimate(flops=30*10**9,bytes_accessed=20*10**6,transcendentals=0)

def permute_rows(order_ref, src, dst, width, scatter, unroll=32):
    def body(i, c):
        for u in range(unroll):
            p=i*unroll+u
            t=order_ref[p]
            a,b=(t,p) if scatter else (p,t)
            dst[pl.ds(a*width,width),:]=src[pl.ds(b*width,width),:]
        return c
    lax.fori_loop(0,N//unroll,body,0)

def load_keys(t, to, rows, neigh_ref):
    for j in range(NB):
        to[pl.ds(j*T,T),:]=rows[pl.ds(pl.multiple_of(neigh_ref[t*NB+j]*T,T),T),:]

def scores_ready(t, qp_ref, kp_ref, kc, neigh_ref):
    load_keys(t,kc,kp_ref,neigh_ref)
    kc[pl.ds(KC,KP-KC),:]=kc[pl.ds(KC-(KP-KC),KP-KC),:]
    return qp_ref[pl.ds(pl.multiple_of(t*T,T),T),:]

def k1(order_ref, neigh_ref, turn_ref, qkv_ref, att_ref, qp_ref, kp_ref, vp_ref, o_ref, rinv_ref, e_ref, tok, per, kc, vc, held, sb, mx):
    i=pl.program_id(0)
    R=U1*T
    @pl.when(i==0)
    def _():
        for j in range(3):
            for s in range(16):
                tok[pl.ds(s*216*PITCH1+j,216,stride=PITCH1),:]=qkv_ref[s,j].astype(f32)
        permute_rows(order_ref,tok,per,PITCH1,False)
        for j,r in enumerate((qp_ref,kp_ref,vp_ref)):
            for u in range(NT):
                r[pl.ds(u*T,T),:]=per[pl.ds(u*T*PITCH1+j,T,stride=PITCH1),:].astype(bf)
        vc[pl.ds(KC,KP-KC),:]=jnp.zeros((KP-KC,HD),bf)
        q=scores_ready(0,qp_ref,kp_ref,kc,neigh_ref)
        s=lax.dot_general(q,kc[...],(((1,),(1,)),((),())),preferred_element_type=f32)
        sb[0]=s
        top=s[:,:HD]
        for b in range(1,KP//HD):
            top=jnp.maximum(top,s[:,b*HD:(b+1)*HD])
        mx[0]=top
    back=jnp.maximum(i-1,0)*R
    for p in range(R):
        tok[pl.ds(order_ref[back+p],1),:]=held[pl.ds(p,1),:]
    for u in range(2):
        t=2*i+u
        load_keys(t,vc,vp_ref,neigh_ref)
        nq=scores_ready(jnp.minimum(t+1,NT-1),qp_ref,kp_ref,kc,neigh_ref)
        mc=jnp.max(mx[u],axis=-1,keepdims=True)*(SC*LOG2E)
        total=jnp.zeros((T,HD),f32)
        o=jnp.zeros((T,HD),f32)
        top=None
        for b in range(BLOCKS):
            cols=pl.ds(b*BW,BW)
            s=lax.dot_general(nq,kc[cols,:],(((1,),(1,)),((),())),preferred_element_type=f32)
            sb[1-u,:,cols]=s
            part=jnp.maximum(s[:,:HD],s[:,HD:])
            top=part if top is None else jnp.maximum(top,part)
            e=jnp.exp2(sb[u,:,cols]*(SC*LOG2E)-mc)
            right=e[:,HD:]
            if b==BLOCKS-1:
                right=jnp.where(lax.broadcasted_iota(jnp.int32,(T,HD),1)<KC%HD,right,0.0)
            total=total+(e[:,:HD]+right)
            eb=e.astype(bf)
            e_ref[u,:,cols]=eb
            o=o+jnp.dot(eb,vc[cols,:],preferred_element_type=f32)
        mx[1-u]=top
        rinv=1.0/jnp.sum(total,axis=-1,keepdims=True)
        o=o*rinv
        rinv_ref[pl.ds(u*T,T),:]=jnp.broadcast_to(rinv,(T,HD))
        o_ref[pl.ds(u*T,T),:]=o
        held[pl.ds(u*T,T),:]=o
    @pl.when(i==NT//U1-1)
    def _():
        def last(c,_):
            for w in range(32):
                p=c*32+w
                tok[pl.ds(order_ref[N-R+p],1),:]=held[pl.ds(p,1),:]
            return _
        lax.fori_loop(0,R//32,last,0)
        for s in range(16):
            att_ref[s]=pltpu.roll(tok[pl.ds(s*216,216),:],lax.rem(HD-turn_ref[0],HD),1).astype(bf)

def run_k1(order, neigh, turn, qkv):
    full=lambda shape: pl.BlockSpec(shape,lambda t,*_:(0,)*len(shape))
    return pl.pallas_call(k1,
      grid_spec=pltpu.PrefetchScalarGridSpec(num_scalar_prefetch=3,grid=(NT//U1,),
        in_specs=[full((16,3,216,HD))],
        out_specs=[full((16,216,HD)),full((N,HD)),full((N,HD)),full((N,HD)),pl.BlockSpec((U1*T,HD),lambda t,*_:(t,0)),
                   pl.BlockSpec((U1*T,HD),lambda t,*_:(t,0)),pl.BlockSpec((U1,T,KP),lambda t,*_:(t,0,0))],
        scratch_shapes=[pltpu.VMEM((N*PITCH1+SPARE,HD),f32),pltpu.VMEM((N*PITCH1+SPARE,HD),f32),pltpu.VMEM((KP,HD),bf),pltpu.VMEM((KP,HD),bf),pltpu.VMEM((U1*T+SPARE,HD),f32),pltpu.VMEM((2,T,KP),f32),pltpu.VMEM((2,T,HD),f32)]),
      out_shape=[jax.ShapeDtypeStruct((16,216,HD),bf)]+[jax.ShapeDtypeStruct((N,HD),bf)]*3+[jax.ShapeDtypeStruct((N,HD),f32),jax.ShapeDtypeStruct((N,HD),f32),jax.ShapeDtypeStruct((NT,T,KP),bf)],
      compiler_params=pltpu.CompilerParams(vmem_limit_bytes=60*1024*1024),
      cost_estimate=COST,name="attend")(order,neigh,turn,qkv)

def k2(order_ref, neigh_ref, turn_ref, g_ref, qp_ref, kp_ref, vp_ref, o_ref, rinv_ref, e_ref, out_ref, tok, gp, acc, kc, vc):
    i=pl.program_id(0)
    R=U2*T
    @pl.when(i==0)
    def _():
        for s in range(16):
            tok[pl.ds(s*216,216),:]=pltpu.roll(g_ref[s].astype(f32),turn_ref[0],1)
        def first(c,_):
            for w in range(32):
                p=c*32+w
                gp[pl.ds(p,1),:]=tok[pl.ds(order_ref[p],1),:]
            return _
        lax.fori_loop(0,R//32,first,0)
        for u in range(NT):
            for j in (1,2):
                acc[pl.ds(u*T*PITCH+j,T,stride=PITCH),:]=jnp.zeros((T,HD),f32)
    g=gp[pl.ds(0,R),:]
    ahead=jnp.minimum((i+1)*R,N-R)
    for p in range(R):
        gp[pl.ds(p,1),:]=tok[pl.ds(order_ref[ahead+p],1),:]
    gs_all=(g*rinv_ref[...]).astype(bf)
    d_all=jnp.sum(gs_all.astype(f32)*o_ref[...],axis=-1,keepdims=True)
    for u in range(U2):
        t=i*U2+u
        ns=[]
        for j in range(NB):
            n=neigh_ref[t*NB+j]
            off=pl.multiple_of(n*T,T); ns.append(n)
            kc[u,pl.ds(j*T,T),:]=kp_ref[pl.ds(off,T),:]
            vc[u,pl.ds(j*T,T),:]=vp_ref[pl.ds(off,T),:]
        q=qp_ref[pl.ds(u*T,T),:]
        gs=gs_all[u*T:(u+1)*T]
        d=d_all[u*T:(u+1)*T]
        dp=lax.dot_general(gs,vc[u],(((1,),(1,)),((),())),preferred_element_type=f32)
        eb=e_ref[u,:,:KC]
        ds=(eb.astype(f32)*(dp-d)).astype(bf)
        dq=jnp.dot(ds,kc[u],preferred_element_type=f32)
        acc[pl.ds(t*T*PITCH,T,stride=PITCH),:]=dq
        dk=lax.dot_general(ds,q,(((0,),(0,)),((),())),preferred_element_type=f32)
        dv=lax.dot_general(eb,gs,(((0,),(0,)),((),())),preferred_element_type=f32)
        for j in range(NB):
            base=ns[j]*(T*PITCH)
            i1=pl.ds(base+1,T,stride=PITCH); i2=pl.ds(base+2,T,stride=PITCH)
            acc[i1,:]=acc[i1,:]+dk[j*T:(j+1)*T]
            acc[i2,:]=acc[i2,:]+dv[j*T:(j+1)*T]
    @pl.when(i==NT//U2-1)
    def _():
        permute_rows(order_ref,acc,tok,PITCH,True)
        for s in range(16):
            for j in range(3):
                rows=tok[pl.ds(s*216*PITCH+j,216,stride=PITCH),:]
                out_ref[s,j]=(rows*SC if j<2 else rows).astype(bf)

def run_k2(order, neigh, turn, g, qp,kp,vp,o,rinv,e):
    full=lambda shape: pl.BlockSpec(shape,lambda t,*_:(0,)*len(shape))
    row=pl.BlockSpec((U2*T,HD),lambda t,*_:(t,0))
    return pl.pallas_call(k2,
      grid_spec=pltpu.PrefetchScalarGridSpec(num_scalar_prefetch=3,grid=(NT//U2,),
        in_specs=[full((16,216,HD)),row,full((N,HD)),full((N,HD)),row,
                   row,pl.BlockSpec((U2,T,KP),lambda t,*_:(t,0,0))],
        out_specs=full((16,3,216,HD)),
        scratch_shapes=[pltpu.VMEM((N*PITCH+SPARE,HD),f32),pltpu.VMEM((U2*T+SPARE,HD),f32),pltpu.VMEM((N*PITCH+SPARE,HD),f32),pltpu.VMEM((U2,KC,HD),bf),pltpu.VMEM((U2,KC,HD),bf)]),
      out_shape=jax.ShapeDtypeStruct((16,3,216,HD),bf),
      compiler_params=pltpu.CompilerParams(vmem_limit_bytes=60*1024*1024),
      cost_estimate=COST,name="attend_grad")(order,neigh,turn,g,qp,kp,vp,o,rinv,e)


def rows_kernel(y_ref, cot_ref, near, near_after, low_half, high_half, near_before, far, far_after, far_before, grad_ref, w_ref):
    cot = cot_ref[...]
    for r in range(4):
        for zl in range(2):
            at = {0: 0, 1: 2, 3: 4}.get(r, 0) + zl
            if r == 2:
                opposite = high_half[3] if zl else low_half[3]
                parts = [far[zl], far_after[zl], opposite, far_before[zl]]
            else:
                opposite = low_half[at] if at < 3 else high_half[at - 3]
                parts = [near[at], near_after[at], opposite, near_before[at]]
            head = lax.rem(y_ref[0] + r, 4) * 2 + zl
            for d in range(4):
                w_ref[head, pl.ds(d * 32, 32), :] = parts[d]
            grad_ref[head] = lax.dot_general(
                cot, w_ref[head], (((1,), (1,)), ((), ())), preferred_element_type=f32
            ).astype(bf)


def run_rows(y, cot, near, far):
    whole = pl.BlockSpec(memory_space=pltpu.VMEM)
    return pl.pallas_call(
        rows_kernel,
        in_specs=[pl.BlockSpec(memory_space=pltpu.SMEM)] + [whole] * 9,
        out_specs=[whole, whole],
        out_shape=[
            jax.ShapeDtypeStruct((8, 432, HD), bf),
            jax.ShapeDtypeStruct((8, HD, 2048), bf),
        ],
        compiler_params=pltpu.CompilerParams(vmem_limit_bytes=40 * 1024 * 1024),
        cost_estimate=pl.CostEstimate(flops=5 * 10**9, bytes_accessed=10**7, transcendentals=0),
        name="grad_rows",
    )(y, cot, *near, *far)


CHIPS = ("y", "zl")
SEQ = ("y", "zl", "c")
VIDEOS = ("x", "zh")


def shift(value, axis, size, step):
    return lax.ppermute(value, axis, [(i, (i + step) % size) for i in range(size)])


def in_place(axis, own, other):
    low = lax.axis_index(axis) == 0
    return jnp.concatenate([jnp.where(low, own, other), jnp.where(low, other, own)], axis=0)


def around(value, axis):
    half = value.shape[0] // 2
    after, before = shift(value, axis, 4, -1), shift(value, axis, 4, 1)
    far = [shift(after[:half], axis, 4, -1), shift(before[half:], axis, 4, 1)]
    return [after, jnp.concatenate(far, axis=0), before]


def gather_weight(own, qkv):
    def along_z(value):
        next_zh, next_zl, next_both = (
            lax.ppermute(value, ("zl", "zh"), [(i, i ^ flip) for i in range(4)]) for flip in (1, 2, 3)
        )
        return in_place(
            "zl", in_place("zh", value, next_zh)[None], in_place("zh", next_zl, next_both)[None]
        )

    opposite = shift(own, "y", 4, 2)
    w = along_z(own)
    y = lax.axis_index("y")
    ring = jnp.stack([w, shift(w, "y", 4, -1), along_z(opposite), shift(w, "y", 4, 1)])
    ring = jnp.concatenate([ring, ring], axis=0)
    w = lax.dynamic_slice_in_dim(ring, 4 - y, 4, 0).reshape(8, 32, 2048)
    w, qkv = lax.optimization_barrier((w, qkv))
    return jnp.concatenate([w] + around(w, "x"), axis=1), qkv


def low(value):
    return value.astype(bf)


def sum_last(rows, grads):
    def at(value, index):
        return lax.dynamic_index_in_dim(value, index, 0, keepdims=False)

    y, z = lax.axis_index("y"), lax.axis_index(("zl", "zh"))
    rows = rows.reshape(4, 4, 16, 2048)
    got = [shift(at(rows, (y + d) % 4), "y", 4, d) for d in (1, 2, 3)]
    *got, grads = lax.optimization_barrier((*got, grads))
    rows = low(sum((part.astype(f32) for part in got), at(rows, y).astype(f32)))
    total = at(rows, z).astype(f32)
    for flip in (1, 2, 3):
        pairs = [(i, i ^ flip) for i in range(4)]
        total = total + lax.ppermute(at(rows, z ^ flip), ("zl", "zh"), pairs).astype(f32)
    return low(total), grads


def local(queries, key_vectors, values, out_weight, cotangent, neighbours, tile_order):
    core = lax.axis_index("c")
    turn = (lax.axis_index("x") * 32).astype(jnp.int32).reshape(1)
    neigh = neighbours.reshape(-1)

    def by_head(tensor):
        return tensor.reshape(216, 16, HD).transpose(1, 0, 2)

    qkv = jnp.stack([by_head(queries[0]), by_head(key_vectors[0]), by_head(values[0])], axis=1)
    cot = cotangent[0]
    weight, qkv = gather_weight(out_weight, qkv)
    weight = weight.reshape(1024, 2048)
    qkv = lax.all_to_all(qkv, SEQ, split_axis=0, concat_axis=0, tiled=True)

    def of_chip(mine, theirs=None):
        theirs = shift(mine, "c", 2, 1) if theirs is None else theirs
        return jnp.concatenate(
            [jnp.where(core == 0, mine, theirs), jnp.where(core == 0, theirs, mine)], axis=0
        )

    cot_chip = of_chip(cot)
    grad = lax.dot_general(
        cot_chip, weight, (((1,), (1,)), ((), ())), preferred_element_type=f32
    ).astype(bf)
    grad = grad.reshape(432, 8, HD).transpose(1, 0, 2)
    grad, qkv = lax.optimization_barrier((grad, qkv))
    grad = lax.all_to_all(grad, CHIPS, split_axis=0, concat_axis=0, tiled=True)

    att, *saved = run_k1(tile_order, neigh, turn, qkv)
    att, grad, cot = lax.optimization_barrier((att, grad, cot))
    cots = [shift(cot, "x", 4, d) for d in (1, 2, 3)]
    att = lax.all_to_all(att.reshape(8, 432, HD), CHIPS, split_axis=0, concat_axis=0, tiled=True)
    att = att.transpose(1, 0, 2).reshape(432, 1024)
    grads = run_k2(tile_order, neigh, turn, grad.reshape(16, 216, HD), *saved)
    att, grads, *cots = lax.optimization_barrier((att, grads, *cots))
    grads = lax.all_to_all(grads, SEQ, split_axis=0, concat_axis=0, tiled=True)

    first_other = shift(cots[0], "c", 2, 1)
    att, first_other = lax.optimization_barrier((att, first_other))
    shares = att.reshape(432, 8, 4, 32).transpose(2, 0, 1, 3).reshape(4, 432, 256)
    shares = [shares[0]] + [shift(shares[d], "x", 4, d) for d in (1, 2, 3)]
    rows = jnp.zeros((256, 2048), f32)
    for share, rows_of in zip(shares, [cot_chip, of_chip(cots[0], first_other), of_chip(cots[1]), of_chip(cots[2])]):
        rows = rows + lax.dot_general(
            share, rows_of, (((0,), (0,)), ((), ())), preferred_element_type=f32
        )
    rows = low(rows).reshape(16, 16, 2048)
    partial = jnp.dot(att, weight, preferred_element_type=f32)
    mine = lax.dynamic_slice_in_dim(partial, core * 216, 216, 0)
    other = lax.dynamic_slice_in_dim(partial, (1 - core) * 216, 216, 0).astype(bf)
    projected = (mine + shift(other, "c", 2, 1).astype(f32)).astype(bf)
    grad_weight, grads = sum_last(rows, grads)

    def by_token(tensor):
        return tensor.transpose(1, 0, 2).reshape(1, 216, 2048)

    return (
        projected[None],
        by_token(grads[:, 0]),
        by_token(grads[:, 1]),
        by_token(grads[:, 2]),
        grad_weight,
    )


def solution(mesh):
    fine = Mesh(np.asarray(mesh.devices).reshape(4, 2, 2, 4, 2), ("y", "zl", "c", "x", "zh"))
    rows = P(VIDEOS, SEQ, None)
    weight = P(SEQ + VIDEOS, None)
    return jax.shard_map(
        local,
        mesh=fine,
        in_specs=(rows, rows, rows, weight, rows, P(), P()),
        out_specs=(rows, rows, rows, rows, weight),
        check_vma=False,
    )
```
